32 devices in a mesh: dp: 8 (over z, y), head: 4 (over x, core).
Axes of the slice: x: 2, y: 2, z: 4, core: 2. Of those that a mesh axis runs over, the one named last changes fastest.
Arguments:
- qkv_raw: bfloat16 [8, 3, 512, 3072], P('dp', None, 'head'), may hold values from -6 to 6
- out_grad: bfloat16 [8, 512, 3072], P('dp', 'head')
- q_gain: float32 [128], replicated, may hold values from 0.25 to 1.75
- k_gain: float32 [128], replicated, may hold values from 0.25 to 1.75
- block_cols: int32 [24, 4, 4], replicated, may hold values from 0 to 3, as said below
- block_count: int32 [24, 4], replicated, may hold values from 1 to 4, as said below
Outputs:
- qkv_grad: bfloat16 [8, 3, 512, 3072], P('dp', None, 'head')
- attn_out: bfloat16 [8, 512, 3072], P('dp', 'head')
- gain_grad: float32 [2, 128], replicated
The draws below stay inside these ranges and needn't reach their ends.
Inputs may be any that keep to these rules, and one draw needn't show every extreme that they name: `block_cols`: for every head and query block the 4 listed key blocks are distinct. `block_count`: some entry equals 4; heads differ in how many blocks they use.
All inputs are finite; a program needn't handle non-finite values.
Results may differ from the reference program's by a relative error of at most 0.008.
Values may be sent and summed in bfloat16 or wider, within the bound.
A program may use at most 64 MiB of HBM per device.

```python
import jax
import jax.numpy as jnp
from jax import lax

HEADS = 24
HD = 128
D = 3072
BLK = 128
KMAX = 4
L = 512
QBLK = 4
CLIPS = 8


def draw_block_cols(key, part):
    key = jax.random.fold_in(key, 11)
    scores = jax.random.randint(key, (HEADS, QBLK, QBLK), 0, 4096) * QBLK + jnp.arange(QBLK)[None, None, :]
    ranked = jnp.argsort(scores, axis=-1, stable=True)
    return ranked[:, :, :KMAX].astype(jnp.int32)


def draw_block_count(key, part):
    key = jax.random.fold_in(key, 12)
    first, second, third, fourth = jax.random.split(key, 4)
    levels = jax.random.randint(first, (HEADS,), 1, KMAX + 1)
    heavy = jax.random.randint(second, (), 0, HEADS)
    levels = jnp.where(jnp.arange(HEADS) == heavy, KMAX, levels)
    drops = jax.random.randint(third, (HEADS, QBLK), 0, 2)
    counts = jnp.maximum(levels[:, None] - drops, 1)
    place = jax.random.randint(fourth, (), 0, QBLK)
    spot = (jnp.arange(HEADS)[:, None] == heavy) & (jnp.arange(QBLK)[None, :] == place)
    return jnp.where(spot, KMAX, counts).astype(jnp.int32)


def draw_out_grad(key, part):
    key = jax.random.fold_in(key, 13)
    shape = (CLIPS, L, HEADS * HD)
    base = jnp.clip(jax.random.normal(key, shape, jnp.float32), -4.0, 4.0)
    clip_pos = jnp.arange(CLIPS).astype(jnp.float32) / max(CLIPS - 1, 1)
    tok_pos = jnp.arange(L).astype(jnp.float32) / (L - 1)
    factor = (1.0 + 2.0 * clip_pos)[:, None, None] * (1.0 + 2.0 * tok_pos)[None, :, None]
    return (base * factor * 0.25).astype(jnp.bfloat16)


def block_scale(key, extent, shards, smallest, top_value):
    level, own = 1.0, jax.random.fold_in(key, 6)
    for dim, parts in shards:
        heights = jnp.exp(jax.random.uniform(jax.random.fold_in(own, dim), (parts,), jnp.float32, smallest / len(shards), top_value / len(shards)))
        level = level * jnp.repeat(heights, extent[dim] // parts).reshape([-1 if axis == dim else 1 for axis in range(len(extent))])
    return level


def centred(rng, dims, spread, reach, cuts=(), dtype=jnp.bfloat16):
    entries = spread * jax.random.normal(rng, dims, jnp.float32)
    if cuts:
        entries = entries * block_scale(rng, dims, cuts, -0.22, 0.18)
    return jnp.clip(entries, -reach, reach).astype(dtype)


def setup_inputs(seed: int = 0) -> dict:
    splits = jax.random.split(jax.random.key(seed), 7)
    return {
        "qkv_raw": centred(splits[0], (CLIPS, 3, L, D), 1.0, 6.0, ((0, 8), (2, 4))),
        "out_grad": draw_out_grad(jax.random.fold_in(splits[6], 71), 0),
        "q_gain": jnp.clip(1.0 + 0.15 * jax.random.normal(splits[2], (HD,), jnp.float32), 0.25, 1.75),
        "k_gain": jnp.clip(1.0 + 0.15 * jax.random.normal(splits[3], (HD,), jnp.float32), 0.25, 1.75),
        "block_cols": draw_block_cols(jax.random.fold_in(splits[6], 71), 0),
        "block_count": draw_block_count(jax.random.fold_in(splits[6], 71), 0),
    }


def normalize(raw_rows, gain):
    widened = raw_rows.astype(jnp.float32)
    inverse = lax.rsqrt(lax.optimization_barrier(jnp.mean(widened * widened, axis=-1, keepdims=True)) + 1e-06)
    unit_rows = widened * inverse
    return (unit_rows, inverse, (unit_rows * gain).astype(jnp.bfloat16))

def norm_backward(grad_rows, unit_rows, inverse, gain):
    widened = grad_rows.astype(jnp.float32)
    scaled = widened * gain
    inner = lax.optimization_barrier(jnp.mean(unit_rows * scaled, axis=-1, keepdims=True))
    grad_raw = (inverse * (scaled - unit_rows * inner)).astype(jnp.bfloat16)
    return (grad_raw, lax.optimization_barrier(jnp.sum(widened * unit_rows, axis=(0, 1))))

def head_pair(queries, key_rows, value_rows, grad_rows, key_cols, counts):
    length = queries.shape[0]
    blocks = length // BLK
    score_scale = HD ** (-0.5)
    query_blocks = queries.reshape(blocks, BLK, HD)
    key_blocks = key_rows.reshape(blocks, BLK, HD)
    value_blocks = value_rows.reshape(blocks, BLK, HD)
    grad_blocks = grad_rows.reshape(blocks, BLK, HD)
    numer = jnp.zeros((blocks, BLK, HD), jnp.float32)
    totals = jnp.zeros((blocks, BLK), jnp.float32)
    for which in range(KMAX):
        column = key_cols[:, which].astype(jnp.int32)
        is_live = (counts > which).astype(jnp.float32)
        key_block = jnp.take(key_blocks, column, axis=0)
        value_block = jnp.take(value_blocks, column, axis=0)
        scores = jnp.einsum('qad,qbd->qab', query_blocks.astype(jnp.float32), key_block.astype(jnp.float32)) * score_scale
        weights = jnp.exp(scores) * is_live[:, None, None]
        totals = totals + lax.optimization_barrier(jnp.sum(weights, axis=-1))
        numer = numer + jnp.einsum('qab,qbd->qad', weights.astype(jnp.bfloat16).astype(jnp.float32), value_block.astype(jnp.float32))
    output = (numer / totals[:, :, None]).astype(jnp.bfloat16)
    deltas = lax.optimization_barrier(jnp.sum(output.astype(jnp.float32) * grad_blocks.astype(jnp.float32), axis=-1))
    grad_query = jnp.zeros((blocks, BLK, HD), jnp.float32)
    grad_key = jnp.zeros((blocks, BLK, HD), jnp.float32)
    grad_value = jnp.zeros((blocks, BLK, HD), jnp.float32)
    for which in range(KMAX):
        column = key_cols[:, which].astype(jnp.int32)
        is_live = (counts > which).astype(jnp.float32)
        key_block = jnp.take(key_blocks, column, axis=0)
        value_block = jnp.take(value_blocks, column, axis=0)
        scores = jnp.einsum('qad,qbd->qab', query_blocks.astype(jnp.float32), key_block.astype(jnp.float32)) * score_scale
        probs = jnp.exp(scores) / totals[:, :, None] * is_live[:, None, None]
        probs_low = probs.astype(jnp.bfloat16).astype(jnp.float32)
        grad_value = grad_value.at[column].add(jnp.einsum('qab,qad->qbd', probs_low, grad_blocks.astype(jnp.float32)))
        dprob = jnp.einsum('qad,qbd->qab', grad_blocks.astype(jnp.float32), value_block.astype(jnp.float32))
        dscore = (probs * (dprob - deltas[:, :, None])).astype(jnp.bfloat16).astype(jnp.float32)
        grad_query = grad_query + jnp.einsum('qab,qbd->qad', dscore, key_block.astype(jnp.float32)) * score_scale
        grad_key = grad_key.at[column].add(jnp.einsum('qab,qad->qbd', dscore, query_blocks.astype(jnp.float32)) * score_scale)
    shape_back = (length, HD)
    return (output.reshape(shape_back), grad_query.astype(jnp.bfloat16).reshape(shape_back), grad_key.astype(jnp.bfloat16).reshape(shape_back), grad_value.astype(jnp.bfloat16).reshape(shape_back))

def reference(qkv_raw, out_grad, q_gain, k_gain, block_cols, block_count):

    def one_clip(pieces):
        raw_clip, grad_clip = pieces
        raw_heads = raw_clip.reshape(3, L, HEADS, HD)
        unit_query, inv_query, norm_query = normalize(raw_heads[0], q_gain)
        unit_key, inv_key, norm_key = normalize(raw_heads[1], k_gain)
        grad_heads = grad_clip.reshape(L, HEADS, HD)
        per_head = (jnp.swapaxes(norm_query, 0, 1), jnp.swapaxes(norm_key, 0, 1), jnp.swapaxes(raw_heads[2], 0, 1), jnp.swapaxes(grad_heads, 0, 1), block_cols, block_count)
        output, grad_query, grad_key, grad_value = lax.map(lambda items: head_pair(*items), per_head)
        grad_raw_q, gain_q = norm_backward(jnp.swapaxes(grad_query, 0, 1), unit_query, inv_query, q_gain)
        grad_raw_k, gain_k = norm_backward(jnp.swapaxes(grad_key, 0, 1), unit_key, inv_key, k_gain)
        stacked = jnp.stack([grad_raw_q, grad_raw_k, jnp.swapaxes(grad_value, 0, 1)], axis=0).reshape(3, L, D)
        return (stacked, jnp.swapaxes(output, 0, 1).reshape(L, D), gain_q, gain_k)
    qkv_grad, attn_out, gains_q, gains_k = lax.map(one_clip, (qkv_raw, out_grad))
    gain_grad = jnp.stack([lax.optimization_barrier(jnp.sum(gains_q, axis=0)), lax.optimization_barrier(jnp.sum(gains_k, axis=0))], axis=0) / CLIPS
    return (qkv_grad, attn_out, gain_grad)
```

```python
import functools

import jax
import jax.numpy as jnp
from jax import lax
from jax.experimental import pallas as pl
from jax.experimental.pallas import tpu as pltpu
from jax.sharding import PartitionSpec as P

BLK = 128
MESH = pl.DeviceIdType.MESH
NT = (((1,), (1,)), ((), ()))
TN = (((0,), (0,)), ((), ()))


def dot_f32(left, right, dims=(((1,), (0,)), ((), ()))):
    return lax.dot_general(left, right, dims, preferred_element_type=jnp.float32)


def normalize(raw_rows, gain):
    widened = raw_rows.astype(jnp.float32)
    inverse = lax.rsqrt(jnp.mean(widened * widened, axis=-1, keepdims=True) + 1e-06)
    unit_rows = widened * inverse
    return unit_rows, inverse, (unit_rows * gain).astype(jnp.bfloat16)


def norm_backward(grad_rows, unit_rows, inverse, gain):
    widened = grad_rows.astype(jnp.float32)
    scaled = widened * gain
    inner = jnp.mean(unit_rows * scaled, axis=-1, keepdims=True)
    grad_raw = (inverse * (scaled - unit_rows * inner)).astype(jnp.bfloat16)
    return grad_raw, jnp.sum(widened * unit_rows, axis=0, keepdims=True)


def kernel(
    n, dp, slots, clips,
    qkv_hbm, grad_hbm, gains_ref, live_ref,
    dqkv_hbm, out_hbm, gain_out,
    raw_buf, grad_buf, res_buf, res_out, norm_buf, prob_buf, ds_buf, sums, part_dp, part_head,
    fwd_send, fwd_recv, own_sem, back_send, back_recv, own_back, red_send, red_recv,
):
    me = lax.axis_index("head")
    my_dp = lax.axis_index("dp")
    tokens = BLK
    length = n * tokens
    head_dim = raw_buf.shape[-1]
    scale = head_dim ** (-0.5)

    def rows(index):
        return pl.ds(pl.multiple_of(index * tokens, tokens), tokens)

    def cols(head):
        return pl.ds(pl.multiple_of(head * head_dim, head_dim), head_dim)

    def forward_copies(slot, step, source):
        target = lax.rem(me + step, n)
        head = target * slots + slot
        return (
            pltpu.make_async_remote_copy(
                src_ref=qkv_hbm.at[:, :, cols(head)],
                dst_ref=raw_buf.at[slot, :, rows(source), :],
                send_sem=fwd_send.at[slot, step, 0],
                recv_sem=fwd_recv.at[slot, step, 0],
                device_id={"head": target},
                device_id_type=MESH,
            ),
            pltpu.make_async_remote_copy(
                src_ref=grad_hbm.at[:, cols(head)],
                dst_ref=grad_buf.at[slot, rows(source), :],
                send_sem=fwd_send.at[slot, step, 1],
                recv_sem=fwd_recv.at[slot, step, 1],
                device_id={"head": target},
                device_id_type=MESH,
            ),
        )

    def own_copies(slot):
        head = me * slots + slot
        return (
            pltpu.make_async_copy(
                qkv_hbm.at[:, :, cols(head)], raw_buf.at[slot, :, rows(me), :], own_sem.at[slot, 0]
            ),
            pltpu.make_async_copy(
                grad_hbm.at[:, cols(head)], grad_buf.at[slot, rows(me), :], own_sem.at[slot, 1]
            ),
        )

    def back_copies(slot, step, owner):
        target = lax.rem(me + step, n)
        head = owner * slots + slot
        return (
            pltpu.make_async_remote_copy(
                src_ref=res_buf.at[slot, :, rows(target), :],
                dst_ref=dqkv_hbm.at[:, :, cols(head)],
                send_sem=back_send.at[slot, step, 0],
                recv_sem=back_recv.at[slot, step, 0],
                device_id={"head": target},
                device_id_type=MESH,
            ),
            pltpu.make_async_remote_copy(
                src_ref=res_out.at[slot, rows(target), :],
                dst_ref=out_hbm.at[:, cols(head)],
                send_sem=back_send.at[slot, step, 1],
                recv_sem=back_recv.at[slot, step, 1],
                device_id={"head": target},
                device_id_type=MESH,
            ),
        )

    def own_back_copies(slot):
        head = me * slots + slot
        return (
            pltpu.make_async_copy(
                res_buf.at[slot, :, rows(me), :], dqkv_hbm.at[:, :, cols(head)], own_back.at[slot, 0]
            ),
            pltpu.make_async_copy(
                res_out.at[slot, rows(me), :], out_hbm.at[:, cols(head)], own_back.at[slot, 1]
            ),
        )

    barrier = pltpu.get_barrier_semaphore()
    for step in range(1, n):
        pl.semaphore_signal(
            barrier, inc=1, device_id={"head": lax.rem(me + step, n)}, device_id_type=MESH
        )
    for step in range(1, dp):
        pl.semaphore_signal(
            barrier, inc=1, device_id={"dp": lax.rem(my_dp + step, dp)}, device_id_type=MESH
        )
    pl.semaphore_wait(barrier, n - 1 + dp - 1)

    @pl.loop(0, slots)
    def _(slot):
        for step in range(1, n):
            for copy in forward_copies(slot, step, me):
                copy.start()
        for copy in own_copies(slot):
            copy.start()

    sums[...] = jnp.zeros_like(sums)
    q_gain = gains_ref[0:1, :]
    k_gain = gains_ref[1:2, :]

    @pl.loop(0, slots)
    def _(slot):
        for copy in own_copies(slot):
            copy.wait()
        for step in range(1, n):
            for copy in forward_copies(slot, step, lax.rem(me + n - step, n)):
                copy.wait_recv()
        head = me * slots + slot
        norm_buf[0] = normalize(raw_buf[slot, 0], q_gain)[2]
        norm_buf[1] = normalize(raw_buf[slot, 1], k_gain)[2]
        for block in range(n):
            here = slice(block * tokens, (block + 1) * tokens)
            query = norm_buf[0, here]
            grads = grad_buf[slot, here]
            scores = dot_f32(query, norm_buf[1], NT) * scale
            weights = jnp.exp(scores) * live_ref[head, block : block + 1, :]
            total = jnp.sum(weights, axis=-1, keepdims=True)
            inverse = 1.0 / total
            numer = dot_f32(weights.astype(jnp.bfloat16), raw_buf[slot, 2])
            output = (numer * inverse).astype(jnp.bfloat16)
            res_out[slot, here] = output
            delta = jnp.sum(
                output.astype(jnp.float32) * grads.astype(jnp.float32), axis=-1, keepdims=True
            )
            probs = weights * inverse
            prob_buf[here] = probs.astype(jnp.bfloat16)
            dprob = dot_f32(grads, raw_buf[slot, 2], NT)
            dscore = (probs * (dprob - delta)).astype(jnp.bfloat16)
            ds_buf[here] = dscore
            grad_query = (dot_f32(dscore, norm_buf[1]) * scale).astype(jnp.bfloat16)
            unit, inv, _ = normalize(raw_buf[slot, 0, here], q_gain)
            raw_grad, gain_part = norm_backward(grad_query, unit, inv, q_gain)
            res_buf[slot, 0, here] = raw_grad
            sums[0:1] += gain_part
        for block in range(n):
            here = slice(block * tokens, (block + 1) * tokens)
            res_buf[slot, 2, here] = dot_f32(prob_buf[:, here], grad_buf[slot], TN).astype(
                jnp.bfloat16
            )
            grad_key = (dot_f32(ds_buf[:, here], norm_buf[0], TN) * scale).astype(jnp.bfloat16)
            unit, inv, _ = normalize(raw_buf[slot, 1, here], k_gain)
            raw_grad, gain_part = norm_backward(grad_key, unit, inv, k_gain)
            res_buf[slot, 1, here] = raw_grad
            sums[1:2] += gain_part
        for step in range(1, n):
            for copy in back_copies(slot, step, me):
                copy.start()
        for copy in own_back_copies(slot):
            copy.start()

    def reduce_copy(axis, part, step, place, base, size):
        position = my_dp if axis == "dp" else me
        return pltpu.make_async_remote_copy(
            src_ref=sums,
            dst_ref=part.at[place],
            send_sem=red_send.at[base + step],
            recv_sem=red_recv.at[base + step],
            device_id={axis: lax.rem(position + step, size)},
            device_id_type=MESH,
        )

    def reduce_stage(axis, part, position, base, size):
        for step in range(1, size):
            reduce_copy(axis, part, step, position, base, size).start()
        part[position] = sums[...]
        for step in range(1, size):
            copy = reduce_copy(axis, part, step, lax.rem(position + size - step, size), base, size)
            copy.wait_recv()
        for step in range(1, size):
            reduce_copy(axis, part, step, position, base, size).wait_send()
        total = part[0]
        for index in range(1, size):
            total = total + part[index]
        sums[...] = total

    reduce_stage("dp", part_dp, my_dp, 0, dp)
    reduce_stage("head", part_head, me, dp, n)
    gain_out[...] = sums[0:2, :] * (1.0 / clips)

    @pl.loop(0, slots)
    def _(slot):
        for step in range(1, n):
            for copy in forward_copies(slot, step, me):
                copy.wait_send()
            for copy in back_copies(slot, step, me):
                copy.wait_send()
            for copy in back_copies(slot, step, lax.rem(me + n - step, n)):
                copy.wait_recv()
        for copy in own_back_copies(slot):
            copy.wait()


def body(qkv_raw, out_grad, q_gain, k_gain, block_cols, block_count):
    _, _, tokens, width = qkv_raw.shape
    heads, blocks, listed = block_cols.shape
    head_dim = width // heads
    n = lax.axis_size("head")
    dp = lax.axis_size("dp")
    slots = heads // n
    length = n * tokens
    clips = qkv_raw.shape[0] * dp
    used = jnp.arange(listed)[None, None, :] < block_count[:, :, None]
    key_block = jnp.arange(length) // BLK
    live = jnp.any(
        (block_cols[:, :, :, None] == key_block[None, None, None, :]) & used[:, :, :, None], axis=2
    ).astype(jnp.float32)
    gains = jnp.stack([q_gain, k_gain], axis=0)
    dma = pltpu.SemaphoreType.DMA
    vmem = pl.BlockSpec(memory_space=pltpu.VMEM)
    hbm = pl.BlockSpec(memory_space=pl.ANY)
    qkv_grad, attn_out, gain_grad = pl.pallas_call(
        functools.partial(kernel, n, dp, slots, clips),
        out_shape=(
            jax.ShapeDtypeStruct((3, tokens, width), jnp.bfloat16),
            jax.ShapeDtypeStruct((tokens, width), jnp.bfloat16),
            jax.ShapeDtypeStruct((2, head_dim), jnp.float32),
        ),
        in_specs=[hbm, hbm, vmem, vmem],
        out_specs=(hbm, hbm, vmem),
        scratch_shapes=[
            pltpu.VMEM((slots, 3, length, head_dim), jnp.bfloat16),
            pltpu.VMEM((slots, length, head_dim), jnp.bfloat16),
            pltpu.VMEM((slots, 3, length, head_dim), jnp.bfloat16),
            pltpu.VMEM((slots, length, head_dim), jnp.bfloat16),
            pltpu.VMEM((2, length, head_dim), jnp.bfloat16),
            pltpu.VMEM((length, length), jnp.bfloat16),
            pltpu.VMEM((length, length), jnp.bfloat16),
            pltpu.VMEM((8, head_dim), jnp.float32),
            pltpu.VMEM((dp, 8, head_dim), jnp.float32),
            pltpu.VMEM((n, 8, head_dim), jnp.float32),
            dma((slots, n, 2)),
            dma((slots, n, 2)),
            dma((slots, 2)),
            dma((slots, n, 2)),
            dma((slots, n, 2)),
            dma((slots, 2)),
            dma((dp + n,)),
            dma((dp + n,)),
        ],
        compiler_params=pltpu.CompilerParams(
            collective_id=0, has_side_effects=True, vmem_limit_bytes=40 * 2**20
        ),
        cost_estimate=pl.CostEstimate(
            flops=14 * slots * length * length * head_dim,
            bytes_accessed=16 * tokens * width,
            transcendentals=slots * length * length,
        ),
    )(qkv_raw[0], out_grad[0], gains, live)
    return qkv_grad[None], attn_out[None], gain_grad


def solution(mesh):
    placed = (P("dp", None, "head", None), P("dp", "head", None), P(), P(), P(), P())
    return jax.shard_map(
        body,
        mesh=mesh,
        in_specs=placed,
        out_specs=(P("dp", None, "head", None), P("dp", "head", None), P()),
        check_vma=False,
    )
```

```python
import functools

import jax
import jax.numpy as jnp
from jax import lax
from jax.experimental import pallas as pl
from jax.experimental.pallas import tpu as pltpu
from jax.sharding import PartitionSpec as P

BLK = 128
MESH = pl.DeviceIdType.MESH
NT = (((1,), (1,)), ((), ()))
TN = (((0,), (0,)), ((), ()))


def dot_f32(left, right, dims=(((1,), (0,)), ((), ()))):
    return lax.dot_general(left, right, dims, preferred_element_type=jnp.float32)


def normalize(raw_rows, gain):
    widened = raw_rows.astype(jnp.float32)
    inverse = lax.rsqrt(jnp.mean(widened * widened, axis=-1, keepdims=True) + 1e-06)
    unit_rows = widened * inverse
    return unit_rows, inverse, (unit_rows * gain).astype(jnp.bfloat16)


def norm_backward(grad_rows, unit_rows, inverse, gain):
    widened = grad_rows.astype(jnp.float32)
    scaled = widened * gain
    inner = jnp.mean(unit_rows * scaled, axis=-1, keepdims=True)
    grad_raw = (inverse * (scaled - unit_rows * inner)).astype(jnp.bfloat16)
    return grad_raw, jnp.sum(widened * unit_rows, axis=0, keepdims=True)


def pick_lane(values, head):
    lanes = lax.broadcasted_iota(jnp.int32, values.shape, values.ndim - 1)
    chosen = jnp.where(lanes == head, values.astype(jnp.float32), 0.0)
    return jnp.sum(chosen, axis=-1, keepdims=True)


def live_keys(counts, columns, block, length):
    key_block = (lax.broadcasted_iota(jnp.int32, (1, length), 1) // BLK).astype(jnp.float32)
    live = jnp.zeros((1, length), jnp.float32)
    for which in range(columns.shape[1]):
        used = counts[block : block + 1] > which
        wanted = jnp.where(used, columns[block, which : which + 1], -1.0)
        live = live + jnp.where(key_block == wanted, 1.0, 0.0)
    return live


def kernel(
    n, dp, slots, clips,
    qkv_hbm, grad_hbm, q_gain_hbm, k_gain_hbm, cols_hbm, count_hbm,
    dqkv_hbm, out_hbm, gain_out,
    raw_buf, grad_buf, res_buf, res_out, norm_buf, prob_buf, ds_buf, sums, part_dp, part_head,
    q_gain_ref, k_gain_ref, cols_ref, count_ref,
    fwd_send, fwd_recv, own_sem, back_send, back_recv, own_back, red_send, red_recv, small_sem,
):
    me = lax.axis_index("head")
    my_dp = lax.axis_index("dp")
    tokens = BLK
    length = n * tokens
    head_dim = raw_buf.shape[-1]
    scale = head_dim ** (-0.5)

    def rows(index):
        return pl.ds(pl.multiple_of(index * tokens, tokens), tokens)

    def cols(head):
        return pl.ds(pl.multiple_of(head * head_dim, head_dim), head_dim)

    def forward_copies(slot, step, source):
        target = lax.rem(me + step, n)
        head = target * slots + slot
        return (
            pltpu.make_async_remote_copy(
                src_ref=qkv_hbm.at[:, :, cols(head)],
                dst_ref=raw_buf.at[slot, :, rows(source), :],
                send_sem=fwd_send.at[slot, step, 0],
                recv_sem=fwd_recv.at[slot, step, 0],
                device_id={"head": target},
                device_id_type=MESH,
            ),
            pltpu.make_async_remote_copy(
                src_ref=grad_hbm.at[:, cols(head)],
                dst_ref=grad_buf.at[slot, rows(source), :],
                send_sem=fwd_send.at[slot, step, 1],
                recv_sem=fwd_recv.at[slot, step, 1],
                device_id={"head": target},
                device_id_type=MESH,
            ),
        )

    def own_copies(slot):
        head = me * slots + slot
        return (
            pltpu.make_async_copy(
                qkv_hbm.at[:, :, cols(head)], raw_buf.at[slot, :, rows(me), :], own_sem.at[slot, 0]
            ),
            pltpu.make_async_copy(
                grad_hbm.at[:, cols(head)], grad_buf.at[slot, rows(me), :], own_sem.at[slot, 1]
            ),
        )

    def back_copies(slot, step, owner):
        target = lax.rem(me + step, n)
        head = owner * slots + slot
        return (
            pltpu.make_async_remote_copy(
                src_ref=res_buf.at[slot, :, rows(target), :],
                dst_ref=dqkv_hbm.at[:, :, cols(head)],
                send_sem=back_send.at[slot, step, 0],
                recv_sem=back_recv.at[slot, step, 0],
                device_id={"head": target},
                device_id_type=MESH,
            ),
            pltpu.make_async_remote_copy(
                src_ref=res_out.at[slot, rows(target), :],
                dst_ref=out_hbm.at[:, cols(head)],
                send_sem=back_send.at[slot, step, 1],
                recv_sem=back_recv.at[slot, step, 1],
                device_id={"head": target},
                device_id_type=MESH,
            ),
        )

    def own_back_copies(slot):
        head = me * slots + slot
        return (
            pltpu.make_async_copy(
                res_buf.at[slot, :, rows(me), :], dqkv_hbm.at[:, :, cols(head)], own_back.at[slot, 0]
            ),
            pltpu.make_async_copy(
                res_out.at[slot, rows(me), :], out_hbm.at[:, cols(head)], own_back.at[slot, 1]
            ),
        )

    barrier = pltpu.get_barrier_semaphore()
    for step in range(1, n):
        pl.semaphore_signal(
            barrier, inc=1, device_id={"head": lax.rem(me + step, n)}, device_id_type=MESH
        )
    for step in range(1, dp):
        pl.semaphore_signal(
            barrier, inc=1, device_id={"dp": lax.rem(my_dp + step, dp)}, device_id_type=MESH
        )
    pl.semaphore_wait(barrier, n - 1 + dp - 1)

    @pl.loop(0, slots)
    def _(slot):
        for step in range(1, n):
            for copy in forward_copies(slot, step, me):
                copy.start()
        for copy in own_copies(slot):
            copy.start()

    sums[...] = jnp.zeros_like(sums)
    small_copies = [
        pltpu.make_async_copy(source, target, small_sem.at[index])
        for index, (source, target) in enumerate(
            (
                (q_gain_hbm, q_gain_ref),
                (k_gain_hbm, k_gain_ref),
                (cols_hbm, cols_ref),
                (count_hbm, count_ref),
            )
        )
    ]
    for copy in small_copies:
        copy.start()
    for copy in small_copies:
        copy.wait()
    q_gain = q_gain_ref[...]
    k_gain = k_gain_ref[...]

    @pl.loop(0, slots)
    def _(slot):
        for copy in own_copies(slot):
            copy.wait()
        for step in range(1, n):
            for copy in forward_copies(slot, step, lax.rem(me + n - step, n)):
                copy.wait_recv()
        head = me * slots + slot
        counts = pick_lane(count_ref[...], head)
        columns = pick_lane(cols_ref[...], head)
        norm_buf[0] = normalize(raw_buf[slot, 0], q_gain)[2]
        norm_buf[1] = normalize(raw_buf[slot, 1], k_gain)[2]
        for block in range(n):
            here = slice(block * tokens, (block + 1) * tokens)
            query = norm_buf[0, here]
            grads = grad_buf[slot, here]
            scores = dot_f32(query, norm_buf[1], NT) * scale
            weights = jnp.exp(scores) * live_keys(counts, columns, block, length)
            total = jnp.sum(weights, axis=-1, keepdims=True)
            inverse = 1.0 / total
            numer = dot_f32(weights.astype(jnp.bfloat16), raw_buf[slot, 2])
            output = (numer * inverse).astype(jnp.bfloat16)
            res_out[slot, here] = output
            delta = jnp.sum(
                output.astype(jnp.float32) * grads.astype(jnp.float32), axis=-1, keepdims=True
            )
            probs = weights * inverse
            prob_buf[here] = probs.astype(jnp.bfloat16)
            dprob = dot_f32(grads, raw_buf[slot, 2], NT)
            dscore = (probs * (dprob - delta)).astype(jnp.bfloat16)
            ds_buf[here] = dscore
            grad_query = (dot_f32(dscore, norm_buf[1]) * scale).astype(jnp.bfloat16)
            unit, inv, _ = normalize(raw_buf[slot, 0, here], q_gain)
            raw_grad, gain_part = norm_backward(grad_query, unit, inv, q_gain)
            res_buf[slot, 0, here] = raw_grad
            sums[0:1] += gain_part
        for block in range(n):
            here = slice(block * tokens, (block + 1) * tokens)
            res_buf[slot, 2, here] = dot_f32(prob_buf[:, here], grad_buf[slot], TN).astype(
                jnp.bfloat16
            )
            grad_key = (dot_f32(ds_buf[:, here], norm_buf[0], TN) * scale).astype(jnp.bfloat16)
            unit, inv, _ = normalize(raw_buf[slot, 1, here], k_gain)
            raw_grad, gain_part = norm_backward(grad_key, unit, inv, k_gain)
            res_buf[slot, 1, here] = raw_grad
            sums[1:2] += gain_part
        for step in range(1, n):
            for copy in back_copies(slot, step, me):
                copy.start()
        for copy in own_back_copies(slot):
            copy.start()

    def reduce_copy(axis, part, step, place, base, size):
        position = my_dp if axis == "dp" else me
        return pltpu.make_async_remote_copy(
            src_ref=sums,
            dst_ref=part.at[place],
            send_sem=red_send.at[base + step],
            recv_sem=red_recv.at[base + step],
            device_id={axis: lax.rem(position + step, size)},
            device_id_type=MESH,
        )

    def reduce_stage(axis, part, position, base, size):
        for step in range(1, size):
            reduce_copy(axis, part, step, position, base, size).start()
        part[position] = sums[...]
        for step in range(1, size):
            copy = reduce_copy(axis, part, step, lax.rem(position + size - step, size), base, size)
            copy.wait_recv()
        for step in range(1, size):
            reduce_copy(axis, part, step, position, base, size).wait_send()
        total = part[0]
        for index in range(1, size):
            total = total + part[index]
        sums[...] = total

    reduce_stage("dp", part_dp, my_dp, 0, dp)
    reduce_stage("head", part_head, me, dp, n)
    gain_out[...] = sums[0:2, :] * (1.0 / clips)

    @pl.loop(0, slots)
    def _(slot):
        for step in range(1, n):
            for copy in forward_copies(slot, step, me):
                copy.wait_send()
            for copy in back_copies(slot, step, me):
                copy.wait_send()
            for copy in back_copies(slot, step, lax.rem(me + n - step, n)):
                copy.wait_recv()
        for copy in own_back_copies(slot):
            copy.wait()


def body(qkv_raw, out_grad, q_gain, k_gain, block_cols, block_count):
    _, _, tokens, width = qkv_raw.shape
    heads, blocks, listed = block_cols.shape
    head_dim = width // heads
    n = lax.axis_size("head")
    dp = lax.axis_size("dp")
    slots = heads // n
    length = n * tokens
    clips = qkv_raw.shape[0] * dp
    dma = pltpu.SemaphoreType.DMA
    vmem = pl.BlockSpec(memory_space=pltpu.VMEM)
    hbm = pl.BlockSpec(memory_space=pltpu.HBM)
    anywhere = pl.BlockSpec(memory_space=pl.ANY)
    qkv_grad, attn_out, gain_grad = pl.pallas_call(
        functools.partial(kernel, n, dp, slots, clips),
        out_shape=(
            jax.ShapeDtypeStruct((3, tokens, width), jnp.bfloat16),
            jax.ShapeDtypeStruct((tokens, width), jnp.bfloat16),
            jax.ShapeDtypeStruct((2, head_dim), jnp.float32),
        ),
        in_specs=[hbm] * 6,
        out_specs=(anywhere, anywhere, vmem),
        scratch_shapes=[
            pltpu.VMEM((slots, 3, length, head_dim), jnp.bfloat16),
            pltpu.VMEM((slots, length, head_dim), jnp.bfloat16),
            pltpu.VMEM((slots, 3, length, head_dim), jnp.bfloat16),
            pltpu.VMEM((slots, length, head_dim), jnp.bfloat16),
            pltpu.VMEM((2, length, head_dim), jnp.bfloat16),
            pltpu.VMEM((length, length), jnp.bfloat16),
            pltpu.VMEM((length, length), jnp.bfloat16),
            pltpu.VMEM((8, head_dim), jnp.float32),
            pltpu.VMEM((dp, 8, head_dim), jnp.float32),
            pltpu.VMEM((n, 8, head_dim), jnp.float32),
            pltpu.VMEM((1, head_dim), jnp.float32),
            pltpu.VMEM((1, head_dim), jnp.float32),
            pltpu.VMEM((blocks, listed, heads), jnp.int32),
            pltpu.VMEM((blocks, heads), jnp.int32),
            dma((slots, n, 2)),
            dma((slots, n, 2)),
            dma((slots, 2)),
            dma((slots, n, 2)),
            dma((slots, n, 2)),
            dma((slots, 2)),
            dma((dp + n,)),
            dma((dp + n,)),
            dma((4,)),
        ],
        compiler_params=pltpu.CompilerParams(
            collective_id=0, has_side_effects=True, vmem_limit_bytes=50 * 2**20
        ),
        cost_estimate=pl.CostEstimate(
            flops=14 * slots * length * length * head_dim,
            bytes_accessed=16 * tokens * width,
            transcendentals=slots * length * length,
        ),
    )(
        *(
            pltpu.with_memory_space_constraint(operand, pltpu.HBM)
            for operand in (
                qkv_raw[0],
                out_grad[0],
                q_gain.reshape(1, head_dim),
                k_gain.reshape(1, head_dim),
                jnp.transpose(block_cols, (1, 2, 0)),
                block_count.T,
            )
        )
    )
    return qkv_grad[None], attn_out[None], gain_grad


def solution(mesh):
    placed = (P("dp", None, "head", None), P("dp", "head", None), P(), P(), P(), P())
    return jax.shard_map(
        body,
        mesh=mesh,
        in_specs=placed,
        out_specs=(P("dp", None, "head", None), P("dp", "head", None), P()),
        check_vma=False,
    )
```

```python
import functools

import jax
import jax.numpy as jnp
from jax import lax
from jax.experimental import pallas as pl
from jax.experimental.pallas import tpu as pltpu
from jax.sharding import PartitionSpec as P

BLK = 128
MESH = pl.DeviceIdType.MESH
NT = (((1,), (1,)), ((), ()))
TN = (((0,), (0,)), ((), ()))


def dot_f32(left, right, dims=(((1,), (0,)), ((), ()))):
    return lax.dot_general(left, right, dims, preferred_element_type=jnp.float32)


def normalize(raw_rows, gain):
    widened = raw_rows.astype(jnp.float32)
    inverse = lax.rsqrt(jnp.mean(widened * widened, axis=-1, keepdims=True) + 1e-06)
    unit_rows = widened * inverse
    return unit_rows, inverse, (unit_rows * gain).astype(jnp.bfloat16)


def norm_backward(grad_rows, unit_rows, inverse, gain):
    widened = grad_rows.astype(jnp.float32)
    scaled = widened * gain
    inner = jnp.mean(unit_rows * scaled, axis=-1, keepdims=True)
    grad_raw = (inverse * (scaled - unit_rows * inner)).astype(jnp.bfloat16)
    return grad_raw, jnp.sum(widened * unit_rows, axis=0, keepdims=True)


def pick_lane(values, head):
    lanes = lax.broadcasted_iota(jnp.int32, values.shape, values.ndim - 1)
    chosen = jnp.where(lanes == head, values.astype(jnp.float32), 0.0)
    return jnp.sum(chosen, axis=-1, keepdims=True)


def live_keys(counts, columns, block, length):
    key_block = (lax.broadcasted_iota(jnp.int32, (1, length), 1) // BLK).astype(jnp.float32)
    live = jnp.zeros((1, length), jnp.float32)
    for which in range(columns.shape[1]):
        used = counts[block : block + 1] > which
        wanted = jnp.where(used, columns[block, which : which + 1], -1.0)
        live = live + jnp.where(key_block == wanted, 1.0, 0.0)
    return live


def partner(index, bit):
    return index + bit - 2 * bit * lax.rem(index // bit, 2)


def kernel(
    n, dp, slots, clips,
    qkv_hbm, grad_hbm, q_gain_hbm, k_gain_hbm, cols_hbm, count_hbm,
    dqkv_hbm, out_hbm, gain_out,
    raw_buf, grad_buf, res_buf, res_out, norm_buf, prob_buf, ds_buf, sums, part_dp, part_head,
    q_gain_ref, k_gain_ref, cols_ref, count_ref,
    fwd_send, fwd_recv, own_sem, back_send, back_recv, own_back, red_send, red_recv, small_sem,
):
    me = lax.axis_index("head")
    my_dp = lax.axis_index("dp")
    tokens = BLK
    length = n * tokens
    head_dim = raw_buf.shape[-1]
    scale = head_dim ** (-0.5)

    def rows(index):
        return pl.ds(pl.multiple_of(index * tokens, tokens), tokens)

    def cols(head):
        return pl.ds(pl.multiple_of(head * head_dim, head_dim), head_dim)

    def forward_copies(slot, step, source):
        target = lax.rem(me + step, n)
        head = target * slots + slot
        return (
            pltpu.make_async_remote_copy(
                src_ref=qkv_hbm.at[:, :, cols(head)],
                dst_ref=raw_buf.at[slot, :, rows(source), :],
                send_sem=fwd_send.at[slot, step, 0],
                recv_sem=fwd_recv.at[slot, step, 0],
                device_id={"head": target},
                device_id_type=MESH,
            ),
            pltpu.make_async_remote_copy(
                src_ref=grad_hbm.at[:, cols(head)],
                dst_ref=grad_buf.at[slot, rows(source), :],
                send_sem=fwd_send.at[slot, step, 1],
                recv_sem=fwd_recv.at[slot, step, 1],
                device_id={"head": target},
                device_id_type=MESH,
            ),
        )

    def own_copies(slot):
        head = me * slots + slot
        return (
            pltpu.make_async_copy(
                qkv_hbm.at[:, :, cols(head)], raw_buf.at[slot, :, rows(me), :], own_sem.at[slot, 0]
            ),
            pltpu.make_async_copy(
                grad_hbm.at[:, cols(head)], grad_buf.at[slot, rows(me), :], own_sem.at[slot, 1]
            ),
        )

    def back_copies(slot, step, owner):
        target = lax.rem(me + step, n)
        head = owner * slots + slot
        return (
            pltpu.make_async_remote_copy(
                src_ref=res_buf.at[slot, :, rows(target), :],
                dst_ref=dqkv_hbm.at[:, :, cols(head)],
                send_sem=back_send.at[slot, step, 0],
                recv_sem=back_recv.at[slot, step, 0],
                device_id={"head": target},
                device_id_type=MESH,
            ),
            pltpu.make_async_remote_copy(
                src_ref=res_out.at[slot, rows(target), :],
                dst_ref=out_hbm.at[:, cols(head)],
                send_sem=back_send.at[slot, step, 1],
                recv_sem=back_recv.at[slot, step, 1],
                device_id={"head": target},
                device_id_type=MESH,
            ),
        )

    def own_back_copies(slot):
        head = me * slots + slot
        return (
            pltpu.make_async_copy(
                res_buf.at[slot, :, rows(me), :], dqkv_hbm.at[:, :, cols(head)], own_back.at[slot, 0]
            ),
            pltpu.make_async_copy(
                res_out.at[slot, rows(me), :], out_hbm.at[:, cols(head)], own_back.at[slot, 1]
            ),
        )

    barrier = pltpu.get_barrier_semaphore()
    for step in range(1, n):
        pl.semaphore_signal(
            barrier, inc=1, device_id={"head": lax.rem(me + step, n)}, device_id_type=MESH
        )
    bits = [1 << power for power in range(dp.bit_length() - 1)]
    for bit in bits:
        pl.semaphore_signal(
            barrier, inc=1, device_id={"dp": partner(my_dp, bit)}, device_id_type=MESH
        )
    pl.semaphore_wait(barrier, n - 1 + len(bits))

    @pl.loop(0, slots)
    def _(slot):
        for step in range(1, n):
            for copy in forward_copies(slot, step, me):
                copy.start()
        for copy in own_copies(slot):
            copy.start()

    sums[...] = jnp.zeros_like(sums)
    small_copies = [
        pltpu.make_async_copy(source, target, small_sem.at[index])
        for index, (source, target) in enumerate(
            (
                (q_gain_hbm, q_gain_ref),
                (k_gain_hbm, k_gain_ref),
                (cols_hbm, cols_ref),
                (count_hbm, count_ref),
            )
        )
    ]
    for copy in small_copies:
        copy.start()
    for copy in small_copies:
        copy.wait()
    q_gain = q_gain_ref[...]
    k_gain = k_gain_ref[...]

    @pl.loop(0, slots)
    def _(slot):
        for copy in own_copies(slot):
            copy.wait()
        for step in range(1, n):
            for copy in forward_copies(slot, step, lax.rem(me + n - step, n)):
                copy.wait_recv()
        head = me * slots + slot
        counts = pick_lane(count_ref[...], head)
        columns = pick_lane(cols_ref[...], head)
        norm_buf[0] = normalize(raw_buf[slot, 0], q_gain)[2]
        norm_buf[1] = normalize(raw_buf[slot, 1], k_gain)[2]
        for block in range(n):
            here = slice(block * tokens, (block + 1) * tokens)
            query = norm_buf[0, here]
            grads = grad_buf[slot, here]
            scores = dot_f32(query, norm_buf[1], NT) * scale
            weights = jnp.exp(scores) * live_keys(counts, columns, block, length)
            total = jnp.sum(weights, axis=-1, keepdims=True)
            inverse = 1.0 / total
            numer = dot_f32(weights.astype(jnp.bfloat16), raw_buf[slot, 2])
            output = (numer * inverse).astype(jnp.bfloat16)
            res_out[slot, here] = output
            delta = jnp.sum(
                output.astype(jnp.float32) * grads.astype(jnp.float32), axis=-1, keepdims=True
            )
            probs = weights * inverse
            prob_buf[here] = probs.astype(jnp.bfloat16)
            dprob = dot_f32(grads, raw_buf[slot, 2], NT)
            dscore = (probs * (dprob - delta)).astype(jnp.bfloat16)
            ds_buf[here] = dscore
            grad_query = (dot_f32(dscore, norm_buf[1]) * scale).astype(jnp.bfloat16)
            unit, inv, _ = normalize(raw_buf[slot, 0, here], q_gain)
            raw_grad, gain_part = norm_backward(grad_query, unit, inv, q_gain)
            res_buf[slot, 0, here] = raw_grad
            sums[0:1] += gain_part
        for block in range(n):
            here = slice(block * tokens, (block + 1) * tokens)
            res_buf[slot, 2, here] = dot_f32(prob_buf[:, here], grad_buf[slot], TN).astype(
                jnp.bfloat16
            )
            grad_key = (dot_f32(ds_buf[:, here], norm_buf[0], TN) * scale).astype(jnp.bfloat16)
            unit, inv, _ = normalize(raw_buf[slot, 1, here], k_gain)
            raw_grad, gain_part = norm_backward(grad_key, unit, inv, k_gain)
            res_buf[slot, 1, here] = raw_grad
            sums[1:2] += gain_part
        for step in range(1, n):
            for copy in back_copies(slot, step, me):
                copy.start()
        for copy in own_back_copies(slot):
            copy.start()

    def reduce_copy(axis, part, step, place, base, size):
        return pltpu.make_async_remote_copy(
            src_ref=sums,
            dst_ref=part.at[place],
            send_sem=red_send.at[base + step],
            recv_sem=red_recv.at[base + step],
            device_id={axis: lax.rem(me + step, size)},
            device_id_type=MESH,
        )

    def reduce_stage(axis, part, position, base, size):
        for step in range(1, size):
            reduce_copy(axis, part, step, position, base, size).start()
        part[position] = sums[...]
        for step in range(1, size):
            copy = reduce_copy(axis, part, step, lax.rem(position + size - step, size), base, size)
            copy.wait_recv()
        for step in range(1, size):
            reduce_copy(axis, part, step, position, base, size).wait_send()
        total = part[0]
        for index in range(1, size):
            total = total + part[index]
        sums[...] = total

    for stage, bit in enumerate(bits):
        copy = pltpu.make_async_remote_copy(
            src_ref=sums,
            dst_ref=part_dp.at[stage],
            send_sem=red_send.at[stage],
            recv_sem=red_recv.at[stage],
            device_id={"dp": partner(my_dp, bit)},
            device_id_type=MESH,
        )
        copy.start()
        copy.wait()
        sums[...] += part_dp[stage]
    reduce_stage("head", part_head, me, dp, n)
    gain_out[...] = sums[0:2, :] * (1.0 / clips)

    @pl.loop(0, slots)
    def _(slot):
        for step in range(1, n):
            for copy in forward_copies(slot, step, me):
                copy.wait_send()
            for copy in back_copies(slot, step, me):
                copy.wait_send()
            for copy in back_copies(slot, step, lax.rem(me + n - step, n)):
                copy.wait_recv()
        for copy in own_back_copies(slot):
            copy.wait()


def body(qkv_raw, out_grad, q_gain, k_gain, block_cols, block_count):
    _, _, tokens, width = qkv_raw.shape
    heads, blocks, listed = block_cols.shape
    head_dim = width // heads
    n = lax.axis_size("head")
    dp = lax.axis_size("dp")
    slots = heads // n
    length = n * tokens
    clips = qkv_raw.shape[0] * dp
    dma = pltpu.SemaphoreType.DMA
    vmem = pl.BlockSpec(memory_space=pltpu.VMEM)
    hbm = pl.BlockSpec(memory_space=pltpu.HBM)
    anywhere = pl.BlockSpec(memory_space=pl.ANY)
    qkv_grad, attn_out, gain_grad = pl.pallas_call(
        functools.partial(kernel, n, dp, slots, clips),
        out_shape=(
            jax.ShapeDtypeStruct((3, tokens, width), jnp.bfloat16),
            jax.ShapeDtypeStruct((tokens, width), jnp.bfloat16),
            jax.ShapeDtypeStruct((2, head_dim), jnp.float32),
        ),
        in_specs=[hbm] * 6,
        out_specs=(anywhere, anywhere, vmem),
        scratch_shapes=[
            pltpu.VMEM((slots, 3, length, head_dim), jnp.bfloat16),
            pltpu.VMEM((slots, length, head_dim), jnp.bfloat16),
            pltpu.VMEM((slots, 3, length, head_dim), jnp.bfloat16),
            pltpu.VMEM((slots, length, head_dim), jnp.bfloat16),
            pltpu.VMEM((2, length, head_dim), jnp.bfloat16),
            pltpu.VMEM((length, length), jnp.bfloat16),
            pltpu.VMEM((length, length), jnp.bfloat16),
            pltpu.VMEM((8, head_dim), jnp.float32),
            pltpu.VMEM((dp, 8, head_dim), jnp.float32),
            pltpu.VMEM((n, 8, head_dim), jnp.float32),
            pltpu.VMEM((1, head_dim), jnp.float32),
            pltpu.VMEM((1, head_dim), jnp.float32),
            pltpu.VMEM((blocks, listed, heads), jnp.int32),
            pltpu.VMEM((blocks, heads), jnp.int32),
            dma((slots, n, 2)),
            dma((slots, n, 2)),
            dma((slots, 2)),
            dma((slots, n, 2)),
            dma((slots, n, 2)),
            dma((slots, 2)),
            dma((dp + n,)),
            dma((dp + n,)),
            dma((4,)),
        ],
        compiler_params=pltpu.CompilerParams(
            collective_id=0, has_side_effects=True, vmem_limit_bytes=50 * 2**20
        ),
        cost_estimate=pl.CostEstimate(
            flops=14 * slots * length * length * head_dim,
            bytes_accessed=16 * tokens * width,
            transcendentals=slots * length * length,
        ),
    )(
        *(
            pltpu.with_memory_space_constraint(operand, pltpu.HBM)
            for operand in (
                qkv_raw[0],
                out_grad[0],
                q_gain.reshape(1, head_dim),
                k_gain.reshape(1, head_dim),
                jnp.transpose(block_cols, (1, 2, 0)),
                block_count.T,
            )
        )
    )
    return qkv_grad[None], attn_out[None], gain_grad


def solution(mesh):
    placed = (P("dp", None, "head", None), P("dp", "head", None), P(), P(), P(), P())
    return jax.shard_map(
        body,
        mesh=mesh,
        in_specs=placed,
        out_specs=(P("dp", None, "head", None), P("dp", "head", None), P()),
        check_vma=False,
    )
```

```python
import functools

import jax
import jax.numpy as jnp
from jax import lax
from jax.experimental import pallas as pl
from jax.experimental.pallas import tpu as pltpu
from jax.sharding import PartitionSpec as P

BLK = 128
MESH = pl.DeviceIdType.MESH
NT = (((1,), (1,)), ((), ()))
TN = (((0,), (0,)), ((), ()))


def dot_f32(left, right, dims=(((1,), (0,)), ((), ()))):
    return lax.dot_general(left, right, dims, preferred_element_type=jnp.float32)


def normalize(raw_rows, gain):
    widened = raw_rows.astype(jnp.float32)
    inverse = lax.rsqrt(jnp.mean(widened * widened, axis=-1, keepdims=True) + 1e-06)
    unit_rows = widened * inverse
    return unit_rows, inverse, (unit_rows * gain).astype(jnp.bfloat16)


def norm_backward(grad_rows, unit_rows, inverse, gain):
    widened = grad_rows.astype(jnp.float32)
    scaled = widened * gain
    inner = jnp.mean(unit_rows * scaled, axis=-1, keepdims=True)
    grad_raw = (inverse * (scaled - unit_rows * inner)).astype(jnp.bfloat16)
    return grad_raw, jnp.sum(widened * unit_rows, axis=0, keepdims=True)


def pick_lane(values, head):
    lanes = lax.broadcasted_iota(jnp.int32, values.shape, values.ndim - 1)
    chosen = jnp.where(lanes == head, values.astype(jnp.float32), 0.0)
    return jnp.sum(chosen, axis=-1, keepdims=True)


def live_keys(counts, columns, block, length):
    key_block = (lax.broadcasted_iota(jnp.int32, (1, length), 1) // BLK).astype(jnp.float32)
    live = jnp.zeros((1, length), jnp.float32)
    for which in range(columns.shape[1]):
        used = counts[block : block + 1] > which
        wanted = jnp.where(used, columns[block, which : which + 1], -1.0)
        live = live + jnp.where(key_block == wanted, 1.0, 0.0)
    return live


def partner(index, bit):
    return index + bit - 2 * bit * lax.rem(index // bit, 2)


def kernel(
    n, dp, slots, clips,
    qkv_hbm, grad_hbm, q_gain_hbm, k_gain_hbm, cols_hbm, count_hbm,
    dqkv_hbm, out_hbm, gain_out,
    raw_buf, grad_buf, res_buf, res_out, norm_buf, prob_buf, ds_buf, sums, part_dp, part_head,
    q_gain_ref, k_gain_ref, cols_ref, count_ref,
    fwd_send, fwd_recv, own_sem, back_send, back_recv, own_back, red_send, red_recv, small_sem,
):
    me = lax.axis_index("head")
    my_dp = lax.axis_index("dp")
    tokens = BLK
    length = n * tokens
    head_dim = raw_buf.shape[-1]
    scale = head_dim ** (-0.5)

    def rows(index):
        return pl.ds(pl.multiple_of(index * tokens, tokens), tokens)

    def cols(head):
        return pl.ds(pl.multiple_of(head * head_dim, head_dim), head_dim)

    def forward_copies(slot, step, source):
        target = lax.rem(me + step, n)
        head = target * slots + slot
        return (
            pltpu.make_async_remote_copy(
                src_ref=qkv_hbm.at[:, :, cols(head)],
                dst_ref=raw_buf.at[slot, :, rows(source), :],
                send_sem=fwd_send.at[slot, step, 0],
                recv_sem=fwd_recv.at[slot, step, 0],
                device_id={"head": target},
                device_id_type=MESH,
            ),
            pltpu.make_async_remote_copy(
                src_ref=grad_hbm.at[:, cols(head)],
                dst_ref=grad_buf.at[slot, rows(source), :],
                send_sem=fwd_send.at[slot, step, 1],
                recv_sem=fwd_recv.at[slot, step, 1],
                device_id={"head": target},
                device_id_type=MESH,
            ),
        )

    def own_copies(slot):
        head = me * slots + slot
        return (
            pltpu.make_async_copy(
                qkv_hbm.at[:, :, cols(head)], raw_buf.at[slot, :, rows(me), :], own_sem.at[slot, 0]
            ),
            pltpu.make_async_copy(
                grad_hbm.at[:, cols(head)], grad_buf.at[slot, rows(me), :], own_sem.at[slot, 1]
            ),
        )

    def back_copies(slot, step, owner):
        target = lax.rem(me + step, n)
        head = owner * slots + slot
        return (
            pltpu.make_async_remote_copy(
                src_ref=res_buf.at[slot, :, rows(target), :],
                dst_ref=dqkv_hbm.at[:, :, cols(head)],
                send_sem=back_send.at[slot, step, 0],
                recv_sem=back_recv.at[slot, step, 0],
                device_id={"head": target},
                device_id_type=MESH,
            ),
            pltpu.make_async_remote_copy(
                src_ref=res_out.at[slot, rows(target), :],
                dst_ref=out_hbm.at[:, cols(head)],
                send_sem=back_send.at[slot, step, 1],
                recv_sem=back_recv.at[slot, step, 1],
                device_id={"head": target},
                device_id_type=MESH,
            ),
        )

    def own_back_copies(slot):
        head = me * slots + slot
        return (
            pltpu.make_async_copy(
                res_buf.at[slot, :, rows(me), :], dqkv_hbm.at[:, :, cols(head)], own_back.at[slot, 0]
            ),
            pltpu.make_async_copy(
                res_out.at[slot, rows(me), :], out_hbm.at[:, cols(head)], own_back.at[slot, 1]
            ),
        )

    order = sorted(range(1, n), key=lambda step: abs(2 * step - n))
    barrier = pltpu.get_barrier_semaphore()
    for step in order:
        pl.semaphore_signal(
            barrier, inc=1, device_id={"head": lax.rem(me + step, n)}, device_id_type=MESH
        )
    bits = [1 << power for power in range(dp.bit_length() - 1)]
    for bit in bits:
        pl.semaphore_signal(
            barrier, inc=1, device_id={"dp": partner(my_dp, bit)}, device_id_type=MESH
        )
    @pl.loop(0, slots)
    def _(slot):
        for copy in own_copies(slot):
            copy.start()

    pl.semaphore_wait(barrier, n - 1 + len(bits))

    @pl.loop(0, slots)
    def _(slot):
        for step in order:
            for copy in forward_copies(slot, step, me):
                copy.start()

    sums[...] = jnp.zeros_like(sums)
    small_copies = [
        pltpu.make_async_copy(source, target, small_sem.at[index])
        for index, (source, target) in enumerate(
            (
                (q_gain_hbm, q_gain_ref),
                (k_gain_hbm, k_gain_ref),
                (cols_hbm, cols_ref),
                (count_hbm, count_ref),
            )
        )
    ]
    for copy in small_copies:
        copy.start()
    for copy in small_copies:
        copy.wait()
    q_gain = q_gain_ref[...]
    k_gain = k_gain_ref[...]

    @pl.loop(0, slots)
    def _(slot):
        for copy in own_copies(slot):
            copy.wait()
        for step in order:
            for copy in forward_copies(slot, step, lax.rem(me + n - step, n)):
                copy.wait_recv()
        head = me * slots + slot
        counts = pick_lane(count_ref[...], head)
        columns = pick_lane(cols_ref[...], head)
        norm_buf[0] = normalize(raw_buf[slot, 0], q_gain)[2]
        norm_buf[1] = normalize(raw_buf[slot, 1], k_gain)[2]
        for block in range(n):
            here = slice(block * tokens, (block + 1) * tokens)
            query = norm_buf[0, here]
            grads = grad_buf[slot, here]
            scores = dot_f32(query, norm_buf[1], NT) * scale
            weights = jnp.exp(scores) * live_keys(counts, columns, block, length)
            total = jnp.sum(weights, axis=-1, keepdims=True)
            inverse = 1.0 / total
            numer = dot_f32(weights.astype(jnp.bfloat16), raw_buf[slot, 2])
            output = (numer * inverse).astype(jnp.bfloat16)
            res_out[slot, here] = output
            delta = jnp.sum(
                output.astype(jnp.float32) * grads.astype(jnp.float32), axis=-1, keepdims=True
            )
            probs = weights * inverse
            prob_buf[here] = probs.astype(jnp.bfloat16)
            dprob = dot_f32(grads, raw_buf[slot, 2], NT)
            dscore = (probs * (dprob - delta)).astype(jnp.bfloat16)
            ds_buf[here] = dscore
            grad_query = (dot_f32(dscore, norm_buf[1]) * scale).astype(jnp.bfloat16)
            unit, inv, _ = normalize(raw_buf[slot, 0, here], q_gain)
            raw_grad, gain_part = norm_backward(grad_query, unit, inv, q_gain)
            res_buf[slot, 0, here] = raw_grad
            sums[0:1] += gain_part
        for block in range(n):
            here = slice(block * tokens, (block + 1) * tokens)
            res_buf[slot, 2, here] = dot_f32(prob_buf[:, here], grad_buf[slot], TN).astype(
                jnp.bfloat16
            )
            grad_key = (dot_f32(ds_buf[:, here], norm_buf[0], TN) * scale).astype(jnp.bfloat16)
            unit, inv, _ = normalize(raw_buf[slot, 1, here], k_gain)
            raw_grad, gain_part = norm_backward(grad_key, unit, inv, k_gain)
            res_buf[slot, 1, here] = raw_grad
            sums[1:2] += gain_part
        for step in order:
            for copy in back_copies(slot, step, me):
                copy.start()
        for copy in own_back_copies(slot):
            copy.start()

    def reduce_copy(axis, part, step, place, base, size):
        return pltpu.make_async_remote_copy(
            src_ref=sums,
            dst_ref=part.at[place],
            send_sem=red_send.at[base + step],
            recv_sem=red_recv.at[base + step],
            device_id={axis: lax.rem(me + step, size)},
            device_id_type=MESH,
        )

    def reduce_stage(axis, part, position, base, size):
        for step in range(1, size):
            reduce_copy(axis, part, step, position, base, size).start()
        part[position] = sums[...]
        for step in range(1, size):
            copy = reduce_copy(axis, part, step, lax.rem(position + size - step, size), base, size)
            copy.wait_recv()
        for step in range(1, size):
            reduce_copy(axis, part, step, position, base, size).wait_send()
        total = part[0]
        for index in range(1, size):
            total = total + part[index]
        sums[...] = total

    for stage, bit in enumerate(bits):
        copy = pltpu.make_async_remote_copy(
            src_ref=sums,
            dst_ref=part_dp.at[stage],
            send_sem=red_send.at[stage],
            recv_sem=red_recv.at[stage],
            device_id={"dp": partner(my_dp, bit)},
            device_id_type=MESH,
        )
        copy.start()
        copy.wait()
        sums[...] += part_dp[stage]
    reduce_stage("head", part_head, me, dp, n)
    gain_out[...] = sums[0:2, :] * (1.0 / clips)

    @pl.loop(0, slots)
    def _(slot):
        for step in order:
            for copy in forward_copies(slot, step, me):
                copy.wait_send()
            for copy in back_copies(slot, step, me):
                copy.wait_send()
            for copy in back_copies(slot, step, lax.rem(me + n - step, n)):
                copy.wait_recv()
        for copy in own_back_copies(slot):
            copy.wait()


def body(qkv_raw, out_grad, q_gain, k_gain, block_cols, block_count):
    _, _, tokens, width = qkv_raw.shape
    heads, blocks, listed = block_cols.shape
    head_dim = width // heads
    n = lax.axis_size("head")
    dp = lax.axis_size("dp")
    slots = heads // n
    length = n * tokens
    clips = qkv_raw.shape[0] * dp
    dma = pltpu.SemaphoreType.DMA
    vmem = pl.BlockSpec(memory_space=pltpu.VMEM)
    hbm = pl.BlockSpec(memory_space=pltpu.HBM)
    anywhere = pl.BlockSpec(memory_space=pl.ANY)
    qkv_grad, attn_out, gain_grad = pl.pallas_call(
        functools.partial(kernel, n, dp, slots, clips),
        out_shape=(
            jax.ShapeDtypeStruct((3, tokens, width), jnp.bfloat16),
            jax.ShapeDtypeStruct((tokens, width), jnp.bfloat16),
            jax.ShapeDtypeStruct((2, head_dim), jnp.float32),
        ),
        in_specs=[hbm] * 6,
        out_specs=(anywhere, anywhere, vmem),
        scratch_shapes=[
            pltpu.VMEM((slots, 3, length, head_dim), jnp.bfloat16),
            pltpu.VMEM((slots, length, head_dim), jnp.bfloat16),
            pltpu.VMEM((slots, 3, length, head_dim), jnp.bfloat16),
            pltpu.VMEM((slots, length, head_dim), jnp.bfloat16),
            pltpu.VMEM((2, length, head_dim), jnp.bfloat16),
            pltpu.VMEM((length, length), jnp.bfloat16),
            pltpu.VMEM((length, length), jnp.bfloat16),
            pltpu.VMEM((8, head_dim), jnp.float32),
            pltpu.VMEM((dp, 8, head_dim), jnp.float32),
            pltpu.VMEM((n, 8, head_dim), jnp.float32),
            pltpu.VMEM((1, head_dim), jnp.float32),
            pltpu.VMEM((1, head_dim), jnp.float32),
            pltpu.VMEM((blocks, listed, heads), jnp.int32),
            pltpu.VMEM((blocks, heads), jnp.int32),
            dma((slots, n, 2)),
            dma((slots, n, 2)),
            dma((slots, 2)),
            dma((slots, n, 2)),
            dma((slots, n, 2)),
            dma((slots, 2)),
            dma((dp + n,)),
            dma((dp + n,)),
            dma((4,)),
        ],
        compiler_params=pltpu.CompilerParams(
            collective_id=0, has_side_effects=True, vmem_limit_bytes=50 * 2**20
        ),
        cost_estimate=pl.CostEstimate(
            flops=14 * slots * length * length * head_dim,
            bytes_accessed=16 * tokens * width,
            transcendentals=slots * length * length,
        ),
    )(
        *(
            pltpu.with_memory_space_constraint(operand, pltpu.HBM)
            for operand in (
                qkv_raw[0],
                out_grad[0],
                q_gain.reshape(1, head_dim),
                k_gain.reshape(1, head_dim),
                jnp.transpose(block_cols, (1, 2, 0)),
                block_count.T,
            )
        )
    )
    return qkv_grad[None], attn_out[None], gain_grad


def solution(mesh):
    placed = (P("dp", None, "head", None), P("dp", "head", None), P(), P(), P(), P())
    return jax.shard_map(
        body,
        mesh=mesh,
        in_specs=placed,
        out_specs=(P("dp", None, "head", None), P("dp", "head", None), P()),
        check_vma=False,
    )
```
